32 devices in a mesh: wave: 8 (over z, x), lev: 4 (over y, core).
Axes of the slice: x: 2, y: 2, z: 4, core: 2. Of those that a mesh axis runs over, the one named last changes fastest.
Arguments:
- spectral: bfloat16 [24, 128, 1280], P('lev', 'wave'), may hold values from -0.19921875 to 0.19921875
- legendre: bfloat16 [128, 32, 1280], P('wave', 'lev'), may hold values from -0.15625 to 0.15625
- weights: float32 [32], replicated, may hold values from 4 to 40
- nlon: int32 [32], replicated, may hold values from 20 to 5136, as said below
- assignment: int32 [128], replicated, may hold values from 1 to 1279, as said below
Outputs:
- tendencies: float32 [24, 128, 1280], P('lev', 'wave')
The draws below stay inside these ranges and needn't reach their ends.
Inputs may be any that keep to these rules, and one draw needn't show every extreme that they name: `assignment`: slots 2 i and 2 i + 1 hold m and 1280 - m for some m with 1 <= m < 640; all values are distinct, and m = 1 is always among them. `nlon`: each count is 20 plus four times a whole number; both ends of the range occur in every draw.
All inputs are finite; a program needn't handle non-finite values.
Results may differ from the reference program's by a relative error of at most 0.018.
Values may be sent and summed in bfloat16 or wider, within the bound.
A program may use at most 64 MiB of HBM per device.

```python
import math
import jax
import jax.numpy as jnp
from jax import lax

TRUNC = 1279
KMAX = 1280
MW = 128
COLS = 24
LAT = 32
NLONPAD = 5376
N_WAVE = 8
N_LEV = 4


def draw_assignment(key, part):
    half_count = MW // 2
    pool = jax.random.permutation(key, (TRUNC + 1) // 2 - 1)[:half_count] + 1
    pool = pool.astype(jnp.int32)
    has_one = jnp.any(pool == 1)
    pool = jnp.where(has_one, pool, pool.at[0].set(1))
    second = (TRUNC + 1 - pool).astype(jnp.int32)
    return jnp.stack([pool, second], axis=1).reshape(MW).astype(jnp.int32)


def draw_nlon(key, part):
    first_key, second_key = jax.random.split(jax.random.fold_in(key, 17))
    counts = jax.random.randint(first_key, (LAT,), 0, TRUNC + 1)
    spots = jax.random.permutation(second_key, LAT)
    counts = counts.at[spots[0]].set(TRUNC).at[spots[1]].set(0)
    return (20 + 4 * counts).astype(jnp.int32)


def level_of(stream_key, extent, pieces, least, high):
    factor_of, own = 1.0, jax.random.fold_in(stream_key, 6)
    for axis_at, shards_of in pieces:
        draws = jnp.exp(jax.random.uniform(jax.random.fold_in(own, axis_at), (shards_of,), jnp.float32, least / len(pieces), high / len(pieces)))
        factor_of = factor_of * jnp.repeat(draws, extent[axis_at] // shards_of).reshape([-1 if axis == axis_at else 1 for axis in range(len(extent))])
    return factor_of


def gaussian(key, shape, scale, limit, shards=(), dtype=jnp.bfloat16):
    drawn = scale * jax.random.normal(key, shape, jnp.float32)
    if shards:
        drawn = drawn * level_of(key, shape, shards, -0.22, 0.18)
    return jnp.clip(drawn, -limit, limit).astype(dtype)


def setup_inputs(seed: int = 0) -> dict:
    key_of = jax.random.split(jax.random.key(seed), 6)
    return {
        "spectral": gaussian(key_of[0], (COLS, MW, KMAX), 0.03, 0.19921875, ((0, 4), (1, 8))),
        "legendre": gaussian(key_of[1], (MW, LAT, KMAX), KMAX ** -0.5, 0.15625, ((0, 8), (1, 4))),
        "weights": jnp.clip(jnp.exp(jax.random.uniform(key_of[2], (LAT,), jnp.float32, math.log(4.0), math.log(40.0))), 4.0, 40.0),
        "nlon": draw_nlon(jax.random.fold_in(key_of[5], 71), 0),
        "assignment": draw_assignment(jax.random.fold_in(key_of[5], 71), 0),
    }


def trig_table(count, waves, lon_rows):
    lon_col = lon_rows[:, None]
    phase = (lon_col * waves[None, :]) % count
    angle = (2.0 * math.pi) * phase.astype(jnp.float32) / count.astype(jnp.float32)
    usable = (lon_col < count) & (2 * waves[None, :] < count)
    cosine = jnp.where(usable, jnp.cos(angle), jnp.zeros((), jnp.float32))
    sine = jnp.where(usable, -jnp.sin(angle), jnp.zeros((), jnp.float32))
    return jnp.concatenate([cosine, sine], axis=1).astype(jnp.bfloat16)


def quadratic(grid):
    fields = grid.reshape(grid.shape[0], grid.shape[1] // 3, 3)
    vort = fields[:, :, 0]
    diverg = fields[:, :, 1]
    temper = fields[:, :, 2]
    stacked = jnp.stack([vort * temper, diverg * temper, vort * diverg], axis=-1)
    return stacked.reshape(grid.shape[0], grid.shape[1]).astype(jnp.bfloat16)


def reference(spectral, legendre, weights, nlon, assignment):
    krange = lax.iota(jnp.int32, KMAX)
    live_rows = krange[None, :] <= (TRUNC - assignment)[:, None]
    coeffs = jnp.where(live_rows[None], spectral, jnp.zeros((), jnp.bfloat16))
    by_slot = jnp.transpose(coeffs, (1, 0, 2))

    def synth_one(inputs):
        table_slot, coeff_slot = inputs
        return jnp.dot(table_slot, coeff_slot.T, preferred_element_type=jnp.float32).astype(jnp.bfloat16)

    fourier = lax.map(synth_one, (legendre, by_slot))
    lon_rows = lax.iota(jnp.int32, NLONPAD)
    half_cols = COLS // 2

    def grid_one(inputs):
        four_lat, count, weight = inputs
        pairs = four_lat.reshape(MW, half_cols, 2)
        stacked = jnp.concatenate([pairs[:, :, 0], pairs[:, :, 1]], axis=0)
        table = trig_table(count, assignment, lon_rows)
        grid = 2.0 * jnp.dot(table, stacked, preferred_element_type=jnp.float32)
        products = quadratic(grid)
        back = jnp.dot(table.T, products, preferred_element_type=jnp.float32)
        back = back * (weight / count.astype(jnp.float32))
        joined = jnp.stack([back[:MW], back[MW:]], axis=-1).reshape(MW, COLS)
        return joined.astype(jnp.bfloat16)

    analysed = lax.map(grid_one, (jnp.transpose(fourier, (1, 0, 2)), nlon, weights))
    analysed = jnp.transpose(analysed, (1, 0, 2))

    def direct_one(inputs):
        table_slot, anal_slot, wave = inputs
        bands_table = table_slot.reshape(N_LEV, N_WAVE, KMAX).astype(jnp.float32)
        bands_anal = anal_slot.reshape(N_LEV, N_WAVE, COLS).astype(jnp.float32)
        band_term = jnp.einsum("blc,blk->bck", bands_anal, bands_table)
        band_term = jnp.where((krange <= TRUNC - wave)[None, None, :], band_term, jnp.zeros((), jnp.float32))
        rounded = lax.optimization_barrier(band_term.astype(jnp.bfloat16))
        return jnp.sum(rounded.astype(jnp.float32), axis=0)

    result = lax.map(direct_one, (legendre, analysed, assignment))
    return jnp.transpose(result, (1, 0, 2))
```

```python
import functools
import math

import jax
import jax.numpy as jnp
from jax import lax
from jax.experimental import pallas as pl
from jax.experimental.pallas import tpu as pltpu
from jax.sharding import PartitionSpec as P

TRUNC = 1279
LON_BLOCK = 768
NLONPAD = 5376


def angle_parts(count, waves, starts):
    phase = starts[:, None] % count * waves[None, :] % count
    angle = 2.0 * math.pi * phase.astype(jnp.float32) / count.astype(jnp.float32)
    return (jnp.cos(angle), jnp.sin(angle))


def compose_table(count, waves, coarse_cos, coarse_sin, fine_cos, fine_sin, lon_rows):
    cosine = (
        coarse_cos[:, None, :] * fine_cos[None, :, :]
        - coarse_sin[:, None, :] * fine_sin[None, :, :]
    )
    sine = (
        coarse_sin[:, None, :] * fine_cos[None, :, :]
        + coarse_cos[:, None, :] * fine_sin[None, :, :]
    )
    rows_total = lon_rows.shape[0]
    cosine = cosine.reshape(rows_total, waves.shape[0])
    sine = sine.reshape(rows_total, waves.shape[0])
    usable = (lon_rows[:, None] < count) & (2 * waves[None, :] < count)
    cosine = jnp.where(usable, cosine, jnp.zeros((), jnp.float32))
    sine = jnp.where(usable, -sine, jnp.zeros((), jnp.float32))
    return jnp.concatenate([cosine, sine], axis=1).astype(jnp.bfloat16)


def quadratic(grid):
    fields = grid.reshape(grid.shape[0], grid.shape[1] // 3, 3)
    vort = fields[:, :, 0]
    diverg = fields[:, :, 1]
    temper = fields[:, :, 2]
    stacked = jnp.stack([vort * temper, diverg * temper, vort * diverg], axis=-1)
    return stacked.reshape(grid.shape[0], grid.shape[1]).astype(jnp.bfloat16)


def per_device(spectral, legendre, weights, nlon, assignment):
    wave_index = lax.axis_index("wave")
    lev_index = lax.axis_index("lev")
    slots = legendre.shape[0]
    lat_band = legendre.shape[1]
    kmax_width = legendre.shape[2]
    all_slots = assignment.shape[0]
    own_waves = lax.dynamic_slice_in_dim(assignment, wave_index * slots, slots)
    krange = lax.iota(jnp.int32, kmax_width)
    live_rows = krange[None, :] <= (TRUNC - own_waves)[:, None]
    local = jnp.where(live_rows[None], spectral, jnp.zeros((), jnp.bfloat16))
    spec_all = lax.all_gather(local, "lev", axis=0, tiled=True)
    columns = spec_all.shape[0]
    four_local = jnp.einsum(
        "mlk,cmk->mlc", legendre, spec_all, preferred_element_type=jnp.float32
    ).astype(jnp.bfloat16)
    fourier = lax.all_to_all(four_local, "wave", split_axis=1, concat_axis=0, tiled=True)
    mine = fourier.shape[1]
    half_cols = columns // 2
    fine_rows = lax.iota(jnp.int32, 128)
    coarse_rows = lax.iota(jnp.int32, NLONPAD // 128) * 128
    coarse_step = LON_BLOCK // 128
    lat_index = lev_index * lat_band + wave_index * mine + 0
    count = lax.dynamic_slice_in_dim(nlon, lat_index, 1)[0]
    weight = lax.dynamic_slice_in_dim(weights, lat_index, 1)[0]
    pairs = fourier[:, 0, :].reshape(all_slots, half_cols, 2)
    stacked = jnp.concatenate([pairs[:, :, 0], pairs[:, :, 1]], axis=0)
    fine_cos, fine_sin = angle_parts(count, assignment, fine_rows)
    coarse_cos_all, coarse_sin_all = angle_parts(count, assignment, coarse_rows)

    def lon_block(block_step, total):
        lon_rows = block_step * LON_BLOCK + lax.iota(jnp.int32, LON_BLOCK)
        coarse_cos = lax.dynamic_slice_in_dim(coarse_cos_all, block_step * coarse_step, coarse_step)
        coarse_sin = lax.dynamic_slice_in_dim(coarse_sin_all, block_step * coarse_step, coarse_step)
        table = compose_table(
            count, assignment, coarse_cos, coarse_sin, fine_cos, fine_sin, lon_rows
        )
        grid = 2.0 * jnp.dot(table, stacked, preferred_element_type=jnp.float32)
        products = quadratic(grid)
        return total + lax.dot_general(
            table, products, (((0,), (0,)), ((), ())), preferred_element_type=jnp.float32
        )

    start_total = jnp.zeros((2 * all_slots, half_cols), jnp.float32)
    total = lax.fori_loop(0, NLONPAD // LON_BLOCK, lon_block, start_total)
    back = total * (weight / count.astype(jnp.float32))
    joined = jnp.stack([back[:all_slots], back[all_slots:]], axis=-1).reshape(all_slots, columns)
    analysed_rows = [joined.astype(jnp.bfloat16)]
    analysed = jnp.stack(analysed_rows, axis=1)
    returned = lax.all_to_all(analysed, "wave", split_axis=0, concat_axis=1, tiled=True)
    band_term = jnp.einsum("mlc,mlk->cmk", returned, legendre, preferred_element_type=jnp.float32)
    band_term = jnp.where(live_rows[None], band_term, jnp.zeros((), jnp.float32))
    return lax.psum_scatter(
        band_term.astype(jnp.bfloat16), "lev", scatter_dimension=0, tiled=True
    ).astype(jnp.float32)


MESH = pl.DeviceIdType.MESH
LANE = 128
F32, BF16, I32 = jnp.float32, jnp.bfloat16, jnp.int32
NT = (((1,), (1,)), ((), ()))
NN = (((1,), (0,)), ((), ()))


def dot(a, b, dims):
    return lax.dot_general(a, b, dims, preferred_element_type=F32)


def iota(shape, dim):
    return lax.broadcasted_iota(I32, shape, dim)


def fused_kernel(
    nlon, weights, waves_s, waves_v, spec, leg, out,
    legp, coefx, tab, rmat, fsend, frecv, bsend, brecv,
    ag_send, ag_recv, f_ssem, f_rsem, b_ssem, b_rsem,
):
    n_wave, n_lev = 8, 4
    cols, slots, kmax = spec.shape
    lats = leg.shape[1]
    blocks = kmax // LANE
    places = blocks + 1
    chunks = slots // 4
    me = lax.axis_index("wave")
    lev = lax.axis_index("lev")
    sibling = lev + 1 - 2 * lax.rem(lev, 2)
    across = lax.rem(lev + 2, n_lev)
    far = lax.rem(sibling + 2, n_lev)

    def peer(step):
        return lax.rem(me + step, n_wave)

    barrier = pltpu.get_barrier_semaphore()
    for step in range(1, n_wave):
        pl.semaphore_signal(barrier, inc=1, device_id=(peer(step), lev), device_id_type=MESH)
    for other in (sibling, across):
        pl.semaphore_signal(barrier, inc=1, device_id=(me, other), device_id_type=MESH)

    def lev_copy(band, chunk, target, sem):
        return pltpu.make_async_remote_copy(
            src_ref=legp.at[band, chunk],
            dst_ref=legp.at[band, chunk],
            send_sem=ag_send.at[sem, chunk],
            recv_sem=ag_recv.at[sem, chunk],
            device_id=(me, target),
            device_id_type=MESH,
        )

    own = [waves_s[me * slots + s] for s in range(slots)]

    def pack_chunk(chunk):
        counts = [
            (jnp.full((lats, LANE), TRUNC + 1, I32) - own[2 * i] + (LANE - 1)) // LANE
            for i in (2 * chunk, 2 * chunk + 1)
        ]
        for p in range(places):
            halves = []
            for h in range(2):
                i = 2 * chunk + h
                if p < blocks:
                    first = leg[2 * i, :, p * LANE:(p + 1) * LANE].astype(F32)
                if p > 0:
                    q = blocks - p
                    second = leg[2 * i + 1, :, q * LANE:(q + 1) * LANE].astype(F32)
                if p == 0:
                    halves.append(first)
                elif p == blocks:
                    halves.append(second)
                else:
                    halves.append(jnp.where(counts[h] > p, first, second))
            legp[lev, chunk, :, p * LANE:(p + 1) * LANE] = jnp.concatenate(halves, axis=0).astype(BF16)

    for chunk in range(chunks):
        pack_chunk(chunk)
        if chunk == 0:
            pl.semaphore_wait(barrier, n_wave - 1 + 2)
        lev_copy(lev, chunk, across, 0).start()
        lev_copy(lev, chunk, sibling, 1).start()

    row16 = iota((slots, LANE), 0)
    lane16 = iota((slots, LANE), 1)
    even_row = lax.rem(row16, 2) == 0
    last = jnp.zeros((slots, LANE), I32)
    for s in range(slots):
        last = jnp.where(row16 == s, TRUNC - own[s], last)
    zero16 = jnp.zeros((slots, LANE), F32)
    coefx[...] = jnp.zeros(coefx.shape, BF16)
    rows_at = pl.ds(pl.multiple_of(me * slots, slots), slots)
    for p in range(places):
        q = blocks - p
        live = jnp.where(even_row, p * LANE, q * LANE) + lane16 <= last
        for c in range(cols):
            even = spec[c, :, p * LANE:(p + 1) * LANE].astype(F32) if p < blocks else zero16
            odd = spec[c, :, q * LANE:(q + 1) * LANE].astype(F32) if p > 0 else zero16
            value = jnp.where(live, jnp.where(even_row, even, odd), 0.0)
            coefx[c, rows_at, p * LANE:(p + 1) * LANE] = value.astype(BF16)

    waves = waves_v[...]
    waves_f = waves.astype(F32)

    def forward(chunk):
        lev_copy(across, chunk, across, 0).wait_recv()
        lev_copy(across, chunk, sibling, 2).start()

    def tables(b):
        count = jnp.full((1, LANE), nlon[b * n_wave + me], I32)
        count_f = count.astype(F32)
        inverse = 1.0 / count_f
        row = iota((40, LANE), 0)
        lon = jnp.where(row < 8, row, jnp.where(row < 24, 8 * (row - 8), LANE * (row - 24)))
        whole = lon.astype(F32) * waves_f
        phase = whole - jnp.floor(whole * inverse) * count_f
        phase = jnp.where(phase < 0.0, phase + count_f, phase)
        phase = jnp.where(phase >= count_f, phase - count_f, phase)
        angle = 2.0 * math.pi * phase / count_f
        cosine, sine = jnp.cos(angle), jnp.sin(angle)
        usable = 2 * waves < count
        c8, s8 = cosine[0:8], sine[0:8]
        fine_cos, fine_sin = [], []
        for t in range(16):
            cm, sm = cosine[8 + t:9 + t], sine[8 + t:9 + t]
            fine_cos.append(cm * c8 - sm * s8)
            fine_sin.append(sm * c8 + cm * s8)
        fine_cos = jnp.concatenate(fine_cos, axis=0)
        fine_sin = jnp.concatenate(fine_sin, axis=0)
        for t in range(tab.shape[1] // LANE):
            cq = jnp.where(usable, cosine[24 + t:25 + t], 0.0)
            sq = jnp.where(usable, sine[24 + t:25 + t], 0.0)
            tab[b, t * LANE:(t + 1) * LANE, 0:LANE] = (cq * fine_cos - sq * fine_sin).astype(BF16)
            tab[b, t * LANE:(t + 1) * LANE, LANE:2 * LANE] = (-(sq * fine_cos + cq * fine_sin)).astype(BF16)

    for b in range(n_lev):
        tables(b)
        forward(b)

    depth = n_lev * slots // 2 * lats
    rrow = iota((depth, depth), 0)
    rcol = iota((depth, depth), 1)
    band_c = rcol // (slots // 2 * lats)
    same = (rrow // 32) == lax.rem(rcol, lats)
    base = (band_c // 2) * 16 + lax.rem(band_c, 2) * 4
    for c in range(cols):
        hit = same & (lax.rem(rrow, 32) == base + (c % 2) * 8 + (2 - c // 2))
        rmat[:, c * depth:(c + 1) * depth] = jnp.where(hit, 1.0, 0.0).astype(BF16)

    half = slots // 2 * lats
    coef_all = coefx[...].reshape(cols * LANE, places * LANE)
    yrow = iota((half, LANE), 0) // lats
    ylane = iota((half, LANE), 1)
    mine = (ylane // slots == me) & (lax.rem(ylane, slots) // 2 == yrow)
    srow = iota((n_wave * 8, half), 0)
    scol = iota((n_wave * 8, half), 1)
    same_lat = srow // 8 == lax.rem(scol, lats)

    def synth(band):
        packed = legp[band].reshape(half, places * LANE)
        four = dot(packed, coef_all, NT)
        pick = jnp.where(same_lat & (lax.rem(srow, 8) == band), 1.0, 0.0).astype(BF16)
        parts = [
            jnp.where(mine, four[:, c * LANE:(c + 1) * LANE], 0.0).astype(BF16) for c in range(cols)
        ]
        return dot(pick, jnp.concatenate(parts, axis=1), NN)

    total = synth(lev)
    for chunk in range(chunks):
        lev_copy(sibling, chunk, sibling, 1).wait_recv()
    total = total + synth(sibling)
    total = total + synth(across)
    for chunk in range(chunks):
        lev_copy(far, chunk, sibling, 2).wait_recv()
    total = total + synth(far)
    for j in range(n_wave):
        for f in range(cols // 2):
            fsend[j, f * 16:(f + 1) * 16, :] = jnp.concatenate(
                [
                    total[j * 8:(j + 1) * 8, (2 * f) * LANE:(2 * f + 1) * LANE],
                    total[j * 8:(j + 1) * 8, (2 * f + 1) * LANE:(2 * f + 2) * LANE],
                ],
                axis=0,
            ).astype(BF16)

    def four_copy(step, slot):
        return pltpu.make_async_remote_copy(
            src_ref=fsend.at[peer(step)],
            dst_ref=frecv.at[slot],
            send_sem=f_ssem.at[step],
            recv_sem=f_rsem.at[step],
            device_id=(peer(step), lev),
            device_id_type=MESH,
        )

    def back_copy(step, slot):
        return pltpu.make_async_remote_copy(
            src_ref=bsend,
            dst_ref=brecv.at[slot],
            send_sem=b_ssem.at[step],
            recv_sem=b_rsem.at[step],
            device_id=(peer(step), lev),
            device_id_type=MESH,
        )

    for step in range(1, n_wave):
        four_copy(step, me).start()
    frecv[me] = fsend[me]
    for step in range(1, n_wave):
        four_copy(step, peer(n_wave - step)).wait_recv()

    gathered = jnp.sum(frecv[...].astype(F32), axis=0)
    even_m = lax.rem(waves, 2) == 0
    row8 = iota((8, LANE), 0)
    in_pair = lax.rem(row8, 4)
    nothing = jnp.zeros((8, LANE), F32)
    width = tab.shape[1]
    wrow = iota((8, width), 0)
    wlane = iota((8, width), 1)

    def spread(part, b):
        at = part * 8 + b
        z, v, h = (gathered[f * 16 + at:f * 16 + at + 1] for f in range(3))
        rows = jnp.where(in_pair == 1, v, jnp.where(in_pair == 2, h, z))
        return jnp.where(row8 // 4 == b % 2, rows, 0.0)

    for t in range(n_lev // 2):
        sums = None
        for b in (2 * t, 2 * t + 1):
            re, im = spread(0, b), spread(1, b)
            lhs = jnp.concatenate(
                [
                    jnp.concatenate([jnp.where(even_m, re, 0.0), jnp.where(even_m, 0.0, re), nothing, nothing], axis=0),
                    jnp.concatenate([nothing, nothing, jnp.where(even_m, im, 0.0), jnp.where(even_m, 0.0, im)], axis=0),
                ],
                axis=1,
            ).astype(BF16)
            term = dot(lhs, tab[b], NT)
            sums = term if sums is None else sums + term
        ce, co, se, so = (sums[g * 8:(g + 1) * 8] for g in range(4))
        p, q, s, d = ce + co, ce - co, se + so, se - so

        def product(x):
            return x * pltpu.roll(x, 7, 0)

        p1, p2, p3, p4 = product(p + s), product(p - s), product(q - d), product(q + d)
        count = jnp.where(wrow < 4, nlon[2 * t * n_wave + me], nlon[(2 * t + 1) * n_wave + me])
        quarter = count // 4
        share = jnp.where((wlane == 0) | (wlane == quarter), 0.5, 1.0)
        share = jnp.where(wlane > quarter, 0.0, share)
        a, e, f, g = (p1 + p2) * share, (p3 + p4) * share, (p1 - p2) * share, (p4 - p3) * share
        folded = jnp.concatenate([a + e, a - e, f + g, f - g], axis=0).astype(BF16)
        first = dot(folded, tab[2 * t], NN)
        second = dot(folded, tab[2 * t + 1], NN)
        row_n = jnp.where(row8 < 4, nlon[2 * t * n_wave + me], nlon[(2 * t + 1) * n_wave + me]).astype(F32)
        row_w = jnp.where(row8 < 4, weights[2 * t * n_wave + me], weights[(2 * t + 1) * n_wave + me])
        scale = 4.0 * (row_w / row_n)
        parts = []
        for part in range(2):
            lanes = slice(part * LANE, (part + 1) * LANE)
            both = [
                jnp.where(even_m, x[part * 16:part * 16 + 8, lanes], x[part * 16 + 8:part * 16 + 16, lanes])
                for x in (first, second)
            ]
            parts.append(jnp.where(row8 < 4, both[0], both[1]) * scale)
        bsend[t * 16:(t + 1) * 16, :] = jnp.concatenate(parts, axis=0).astype(BF16)

    for step in range(1, n_wave):
        back_copy(step, me).start()
    brecv[me] = bsend[...]
    for step in range(1, n_wave):
        back_copy(step, peer(n_wave - step)).wait_recv()

    choose = jnp.where(lane16 == me * slots + row16, 1.0, 0.0).astype(BF16)
    turned = dot(choose, brecv[...].reshape(depth, LANE), NT).astype(BF16)
    placed = dot(turned, rmat[...], NN)
    dcol = iota((slots, depth), 1)
    own_pair = lax.rem(dcol // lats, slots // 2) == iota((slots, depth), 0) // 2
    rows = jnp.concatenate(
        [jnp.where(own_pair, placed[:, c * depth:(c + 1) * depth], 0.0) for c in range(cols)], axis=0
    ).astype(BF16)
    result = dot(rows, legp[...].reshape(depth, places * LANE), NN)
    for k in range(blocks):
        live = k * LANE + lane16 <= last
        q = blocks - k
        for c in range(cols):
            even = result[c * slots:(c + 1) * slots, k * LANE:(k + 1) * LANE]
            odd = result[c * slots:(c + 1) * slots, q * LANE:(q + 1) * LANE]
            out[c, :, k * LANE:(k + 1) * LANE] = jnp.where(live, jnp.where(even_row, even, odd), 0.0)

    for chunk in range(chunks):
        lev_copy(lev, chunk, across, 0).wait_send()
        lev_copy(lev, chunk, sibling, 1).wait_send()
        lev_copy(across, chunk, sibling, 2).wait_send()
    for step in range(1, n_wave):
        four_copy(step, me).wait_send()
        back_copy(step, me).wait_send()


def fused(spectral, legendre, weights, nlon, assignment):
    cols, slots, kmax = spectral.shape
    lats = legendre.shape[1]
    packed = kmax + LANE
    depth = 4 * slots // 2 * lats
    quarter = -(-(NLONPAD // 4 + 1) // LANE) * LANE
    smem = pl.BlockSpec(memory_space=pltpu.SMEM)
    vmem = pl.BlockSpec(memory_space=pltpu.VMEM)
    dma = pltpu.SemaphoreType.DMA
    return pl.pallas_call(
        fused_kernel,
        out_shape=jax.ShapeDtypeStruct((cols, slots, kmax), F32),
        in_specs=[smem, smem, smem, vmem, vmem, vmem],
        out_specs=vmem,
        scratch_shapes=[
            pltpu.VMEM((4, slots // 4, 2 * lats, packed), BF16),
            pltpu.VMEM((cols, LANE, packed), BF16),
            pltpu.VMEM((4, quarter, 2 * LANE), BF16),
            pltpu.VMEM((depth, cols * depth), BF16),
            pltpu.VMEM((8, 48, LANE), BF16),
            pltpu.VMEM((8, 48, LANE), BF16),
            pltpu.VMEM((32, LANE), BF16),
            pltpu.VMEM((8, 32, LANE), BF16),
            dma((3, slots // 4)),
            dma((3, slots // 4)),
            dma((8,)),
            dma((8,)),
            dma((8,)),
            dma((8,)),
        ],
        compiler_params=pltpu.CompilerParams(
            collective_id=0, has_side_effects=True, vmem_limit_bytes=48 * 1024 * 1024
        ),
    )(nlon, weights, assignment, assignment.reshape(1, -1), spectral, legendre)


def solution(mesh):
    def per_shard(spectral, legendre, weights, nlon, assignment):
        fits = (
            mesh.shape["wave"] == 8
            and mesh.shape["lev"] == 4
            and spectral.shape[:2] == (6, 16)
            and legendre.shape[:2] == (16, 8)
            and spectral.shape[2] == TRUNC + 1
        )
        plan = fused if fits else per_device
        return plan(spectral, legendre, weights, nlon, assignment)

    return jax.shard_map(
        per_shard,
        mesh=mesh,
        in_specs=(P("lev", "wave", None), P("wave", "lev", None), P(), P(), P()),
        out_specs=P("lev", "wave", None),
        check_vma=False,
    )
```

```python
import functools
import math

import jax
import jax.numpy as jnp
from jax import lax
from jax.experimental import pallas as pl
from jax.experimental.pallas import tpu as pltpu
from jax.sharding import PartitionSpec as P

TRUNC = 1279
LON_BLOCK = 768
NLONPAD = 5376


def angle_parts(count, waves, starts):
    phase = starts[:, None] % count * waves[None, :] % count
    angle = 2.0 * math.pi * phase.astype(jnp.float32) / count.astype(jnp.float32)
    return (jnp.cos(angle), jnp.sin(angle))


def compose_table(count, waves, coarse_cos, coarse_sin, fine_cos, fine_sin, lon_rows):
    cosine = (
        coarse_cos[:, None, :] * fine_cos[None, :, :]
        - coarse_sin[:, None, :] * fine_sin[None, :, :]
    )
    sine = (
        coarse_sin[:, None, :] * fine_cos[None, :, :]
        + coarse_cos[:, None, :] * fine_sin[None, :, :]
    )
    rows_total = lon_rows.shape[0]
    cosine = cosine.reshape(rows_total, waves.shape[0])
    sine = sine.reshape(rows_total, waves.shape[0])
    usable = (lon_rows[:, None] < count) & (2 * waves[None, :] < count)
    cosine = jnp.where(usable, cosine, jnp.zeros((), jnp.float32))
    sine = jnp.where(usable, -sine, jnp.zeros((), jnp.float32))
    return jnp.concatenate([cosine, sine], axis=1).astype(jnp.bfloat16)


def quadratic(grid):
    fields = grid.reshape(grid.shape[0], grid.shape[1] // 3, 3)
    vort = fields[:, :, 0]
    diverg = fields[:, :, 1]
    temper = fields[:, :, 2]
    stacked = jnp.stack([vort * temper, diverg * temper, vort * diverg], axis=-1)
    return stacked.reshape(grid.shape[0], grid.shape[1]).astype(jnp.bfloat16)


def per_device(spectral, legendre, weights, nlon, assignment):
    wave_index = lax.axis_index("wave")
    lev_index = lax.axis_index("lev")
    slots = legendre.shape[0]
    lat_band = legendre.shape[1]
    kmax_width = legendre.shape[2]
    all_slots = assignment.shape[0]
    own_waves = lax.dynamic_slice_in_dim(assignment, wave_index * slots, slots)
    krange = lax.iota(jnp.int32, kmax_width)
    live_rows = krange[None, :] <= (TRUNC - own_waves)[:, None]
    local = jnp.where(live_rows[None], spectral, jnp.zeros((), jnp.bfloat16))
    spec_all = lax.all_gather(local, "lev", axis=0, tiled=True)
    columns = spec_all.shape[0]
    four_local = jnp.einsum(
        "mlk,cmk->mlc", legendre, spec_all, preferred_element_type=jnp.float32
    ).astype(jnp.bfloat16)
    fourier = lax.all_to_all(four_local, "wave", split_axis=1, concat_axis=0, tiled=True)
    mine = fourier.shape[1]
    half_cols = columns // 2
    fine_rows = lax.iota(jnp.int32, 128)
    coarse_rows = lax.iota(jnp.int32, NLONPAD // 128) * 128
    coarse_step = LON_BLOCK // 128
    lat_index = lev_index * lat_band + wave_index * mine + 0
    count = lax.dynamic_slice_in_dim(nlon, lat_index, 1)[0]
    weight = lax.dynamic_slice_in_dim(weights, lat_index, 1)[0]
    pairs = fourier[:, 0, :].reshape(all_slots, half_cols, 2)
    stacked = jnp.concatenate([pairs[:, :, 0], pairs[:, :, 1]], axis=0)
    fine_cos, fine_sin = angle_parts(count, assignment, fine_rows)
    coarse_cos_all, coarse_sin_all = angle_parts(count, assignment, coarse_rows)

    def lon_block(block_step, total):
        lon_rows = block_step * LON_BLOCK + lax.iota(jnp.int32, LON_BLOCK)
        coarse_cos = lax.dynamic_slice_in_dim(coarse_cos_all, block_step * coarse_step, coarse_step)
        coarse_sin = lax.dynamic_slice_in_dim(coarse_sin_all, block_step * coarse_step, coarse_step)
        table = compose_table(
            count, assignment, coarse_cos, coarse_sin, fine_cos, fine_sin, lon_rows
        )
        grid = 2.0 * jnp.dot(table, stacked, preferred_element_type=jnp.float32)
        products = quadratic(grid)
        return total + lax.dot_general(
            table, products, (((0,), (0,)), ((), ())), preferred_element_type=jnp.float32
        )

    start_total = jnp.zeros((2 * all_slots, half_cols), jnp.float32)
    total = lax.fori_loop(0, NLONPAD // LON_BLOCK, lon_block, start_total)
    back = total * (weight / count.astype(jnp.float32))
    joined = jnp.stack([back[:all_slots], back[all_slots:]], axis=-1).reshape(all_slots, columns)
    analysed_rows = [joined.astype(jnp.bfloat16)]
    analysed = jnp.stack(analysed_rows, axis=1)
    returned = lax.all_to_all(analysed, "wave", split_axis=0, concat_axis=1, tiled=True)
    band_term = jnp.einsum("mlc,mlk->cmk", returned, legendre, preferred_element_type=jnp.float32)
    band_term = jnp.where(live_rows[None], band_term, jnp.zeros((), jnp.float32))
    return lax.psum_scatter(
        band_term.astype(jnp.bfloat16), "lev", scatter_dimension=0, tiled=True
    ).astype(jnp.float32)


MESH = pl.DeviceIdType.MESH
LANE = 128
F32, BF16, I32 = jnp.float32, jnp.bfloat16, jnp.int32
NT = (((1,), (1,)), ((), ()))
NN = (((1,), (0,)), ((), ()))


def dot(a, b, dims):
    return lax.dot_general(a, b, dims, preferred_element_type=F32)


def iota(shape, dim):
    return lax.broadcasted_iota(I32, shape, dim)


def fused_kernel(
    nlon_in, weights_in, waves_in, waves_row, spec_in, leg_in, out,
    nlon, weights, waves_s, waves_v, spec, leg,
    legp, coef, tab, rmat, emat, fsend, frecv, bsend, brecv,
    in_sem, ag_send, ag_recv, f_ssem, f_rsem, b_ssem, b_rsem,
):
    n_wave, n_lev = 8, 4
    chunks = leg.shape[0] // 4
    moves = [
        pltpu.make_async_copy(leg_in.at[pl.ds(4 * i, 4)], leg.at[pl.ds(4 * i, 4)], in_sem.at[i])
        for i in range(chunks)
    ]
    small = ((waves_in, waves_s), (spec_in, spec), (waves_row, waves_v), (nlon_in, nlon), (weights_in, weights))
    moves += [pltpu.make_async_copy(a, b, in_sem.at[chunks + i]) for i, (a, b) in enumerate(small)]
    for move in [moves[chunks]] + moves[:chunks] + moves[chunks + 1:]:
        move.start()
    cols, slots, kmax = spec.shape
    lats = leg.shape[1]
    blocks = kmax // LANE
    places = blocks + 1
    me = lax.axis_index("wave")
    lev = lax.axis_index("lev")
    sibling = lev + 1 - 2 * lax.rem(lev, 2)
    across = lax.rem(lev + 2, n_lev)
    far = lax.rem(sibling + 2, n_lev)

    def peer(step):
        return lax.rem(me + step, n_wave)

    barrier = pltpu.get_barrier_semaphore()
    for step in range(1, n_wave):
        pl.semaphore_signal(barrier, inc=1, device_id=(peer(step), lev), device_id_type=MESH)
    for other in (sibling, across):
        pl.semaphore_signal(barrier, inc=1, device_id=(me, other), device_id_type=MESH)

    def lev_copy(band, chunk, target, sem):
        return pltpu.make_async_remote_copy(
            src_ref=legp.at[band, chunk],
            dst_ref=legp.at[band, chunk],
            send_sem=ag_send.at[sem, chunk],
            recv_sem=ag_recv.at[sem, chunk],
            device_id=(me, target),
            device_id_type=MESH,
        )

    moves[chunks].wait()
    own = [waves_s[me * slots + s] for s in range(slots)]

    def pack_chunk(chunk):
        counts = [
            (jnp.full((lats, LANE), TRUNC + 1, I32) - own[2 * i] + (LANE - 1)) >> 7
            for i in (2 * chunk, 2 * chunk + 1)
        ]
        for p in range(places):
            halves = []
            for h in range(2):
                i = 2 * chunk + h
                if p < blocks:
                    first = leg[2 * i, :, p * LANE:(p + 1) * LANE].astype(F32)
                if p > 0:
                    q = blocks - p
                    second = leg[2 * i + 1, :, q * LANE:(q + 1) * LANE].astype(F32)
                if p == 0:
                    halves.append(first)
                elif p == blocks:
                    halves.append(second)
                else:
                    halves.append(jnp.where(counts[h] > p, first, second))
            legp[lev, chunk, :, p * LANE:(p + 1) * LANE] = jnp.concatenate(halves, axis=0).astype(BF16)

    for chunk in range(chunks):
        moves[chunk].wait()
        pack_chunk(chunk)
        if chunk == 0:
            pl.semaphore_wait(barrier, n_wave - 1 + 2)
        lev_copy(lev, chunk, across, 0).start()
        lev_copy(lev, chunk, sibling, 1).start()

    row16 = iota((slots, LANE), 0)
    lane16 = iota((slots, LANE), 1)
    even_row = row16 & 1 == 0
    last = jnp.zeros((slots, LANE), I32)
    for s in range(slots):
        last = jnp.where(row16 == s, TRUNC - own[s], last)
    zero16 = jnp.zeros((slots, LANE), F32)
    moves[chunks + 1].wait()
    padding = jnp.zeros((LANE - cols * slots, LANE), F32)
    for p in range(places):
        q = blocks - p
        live = jnp.where(even_row, p * LANE, q * LANE) + lane16 <= last
        pieces = []
        for c in range(cols):
            even = spec[c, :, p * LANE:(p + 1) * LANE].astype(F32) if p < blocks else zero16
            odd = spec[c, :, q * LANE:(q + 1) * LANE].astype(F32) if p > 0 else zero16
            pieces.append(jnp.where(live, jnp.where(even_row, even, odd), 0.0))
        piece = jnp.concatenate(pieces + [padding], axis=0)
        coef[p * LANE:(p + 1) * LANE, :] = piece.T.astype(BF16)

    for move in moves[chunks + 2:]:
        move.wait()
    waves = waves_v[...]
    waves_f = waves.astype(F32)

    def forward(chunk):
        lev_copy(across, chunk, across, 0).wait_recv()
        lev_copy(across, chunk, sibling, 2).start()

    def tables(b):
        count = jnp.full((1, LANE), nlon[b * n_wave + me], I32)
        count_f = count.astype(F32)
        inverse = 1.0 / count_f
        row = iota((40, LANE), 0)
        lon = jnp.where(row < 8, row, jnp.where(row < 24, 8 * (row - 8), LANE * (row - 24)))
        whole = lon.astype(F32) * waves_f
        phase = whole - jnp.floor(whole * inverse) * count_f
        phase = jnp.where(phase < 0.0, phase + count_f, phase)
        phase = jnp.where(phase >= count_f, phase - count_f, phase)
        angle = 2.0 * math.pi * phase / count_f
        cosine, sine = jnp.cos(angle), jnp.sin(angle)
        usable = 2 * waves < count
        c8, s8 = cosine[0:8], sine[0:8]
        fine_cos, fine_sin = [], []
        for t in range(16):
            cm, sm = cosine[8 + t:9 + t], sine[8 + t:9 + t]
            fine_cos.append(cm * c8 - sm * s8)
            fine_sin.append(sm * c8 + cm * s8)
        fine_cos = jnp.concatenate(fine_cos, axis=0)
        fine_sin = jnp.concatenate(fine_sin, axis=0)
        for t in range(tab.shape[1] // LANE):
            cq = jnp.where(usable, cosine[24 + t:25 + t], 0.0)
            sq = jnp.where(usable, sine[24 + t:25 + t], 0.0)
            tab[b, t * LANE:(t + 1) * LANE, 0:LANE] = (cq * fine_cos - sq * fine_sin).astype(BF16)
            tab[b, t * LANE:(t + 1) * LANE, LANE:2 * LANE] = (-(sq * fine_cos + cq * fine_sin)).astype(BF16)

    for b in range(n_lev):
        tables(b)
        forward(b)

    depth = n_lev * slots // 2 * lats
    rrow = iota((depth, depth), 0)
    rcol = iota((depth, depth), 1)
    band_c = rcol >> 6
    same = (rrow >> 5) == rcol & 7
    base = (band_c >> 1) * 16 + (band_c & 1) * 4
    for c in range(cols):
        hit = same & (rrow & 31 == base + (c % 2) * 8 + (2 - c // 2))
        rmat[:, c * depth:(c + 1) * depth] = jnp.where(hit, 1.0, 0.0).astype(BF16)

    erow = iota((LANE, cols * LANE), 0)
    ecol = iota((LANE, cols * LANE), 1)
    lane_of = ecol & (LANE - 1)
    hit = erow == (ecol >> 7) * slots + (lane_of & (slots - 1))
    emat[...] = jnp.where(hit, 1.0, 0.0).astype(BF16)

    krow, kcol = iota((LANE, LANE), 0), iota((LANE, LANE), 1)
    shift = jnp.where((krow < 32) & (kcol == krow + 32 * lax.rem(me, 4)), 1.0, 0.0).astype(BF16)

    half = slots // 2 * lats
    coef_all = coef[...]
    yrow = iota((half, LANE), 0) >> 3
    ylane = iota((half, LANE), 1)
    mine = (ylane & (slots - 1)) >> 1 == yrow
    srow = iota((n_wave * 8, half), 0)
    scol = iota((n_wave * 8, half), 1)
    same_lat = srow >> 3 == scol & 7

    def synth(band):
        packed = legp[band].reshape(half, places * LANE)
        four = jnp.where(mine, dot(packed, coef_all, NN), 0.0).astype(BF16)
        pick = jnp.where(same_lat & (srow & 7 == band), 1.0, 0.0).astype(BF16)
        return dot(pick, four, NN)

    total = synth(lev)
    for chunk in range(chunks):
        lev_copy(sibling, chunk, sibling, 1).wait_recv()
    total = total + synth(sibling)
    total = total + synth(across)
    for chunk in range(chunks):
        lev_copy(far, chunk, sibling, 2).wait_recv()
    total = total + synth(far)
    for j in range(n_wave):
        fsend[j] = total[j * 8:(j + 1) * 8]

    def four_copy(step, slot):
        return pltpu.make_async_remote_copy(
            src_ref=fsend.at[peer(step)],
            dst_ref=frecv.at[slot],
            send_sem=f_ssem.at[step],
            recv_sem=f_rsem.at[step],
            device_id=(peer(step), lev),
            device_id_type=MESH,
        )

    def back_copy(step, slot):
        return pltpu.make_async_remote_copy(
            src_ref=bsend.at[peer(step)],
            dst_ref=brecv.at[slot],
            send_sem=b_ssem.at[step],
            recv_sem=b_rsem.at[step],
            device_id=(peer(step), lev),
            device_id_type=MESH,
        )

    for step in range(1, n_wave):
        four_copy(step, me).start()
    frecv[me] = fsend[me]
    for step in range(1, n_wave):
        four_copy(step, peer(n_wave - step)).wait_recv()

    wide = dot(frecv[...].reshape(n_wave * 8, LANE).astype(BF16), emat[...], NN)
    from_wave = iota((8, LANE), 1) >> 4
    columns = []
    for c in range(cols):
        part = wide[0:8, c * LANE:(c + 1) * LANE]
        for j in range(1, n_wave):
            part = jnp.where(from_wave == j, wide[j * 8:(j + 1) * 8, c * LANE:(c + 1) * LANE], part)
        columns.append(part)
    even_m = waves & 1 == 0
    row8 = iota((8, LANE), 0)
    in_pair = row8 & 3
    nothing = jnp.zeros((8, LANE), F32)
    width = tab.shape[1]
    wrow = iota((8, width), 0)
    wlane = iota((8, width), 1)

    def spread(part, b):
        z, v, h = (columns[2 * f + part][b:b + 1] for f in range(3))
        rows = jnp.where(in_pair == 1, v, jnp.where(in_pair == 2, h, z))
        return jnp.where(row8 >> 2 == b % 2, rows, 0.0)

    back = []
    for t in range(n_lev // 2):
        sums = None
        for b in (2 * t, 2 * t + 1):
            re, im = spread(0, b), spread(1, b)
            lhs = jnp.concatenate(
                [
                    jnp.concatenate([jnp.where(even_m, re, 0.0), jnp.where(even_m, 0.0, re), nothing, nothing], axis=0),
                    jnp.concatenate([nothing, nothing, jnp.where(even_m, im, 0.0), jnp.where(even_m, 0.0, im)], axis=0),
                ],
                axis=1,
            ).astype(BF16)
            term = dot(lhs, tab[b], NT)
            sums = term if sums is None else sums + term
        ce, co, se, so = (sums[g * 8:(g + 1) * 8] for g in range(4))
        p, q, s, d = ce + co, ce - co, se + so, se - so

        def product(x):
            return x * pltpu.roll(x, 7, 0)

        p1, p2, p3, p4 = product(p + s), product(p - s), product(q - d), product(q + d)
        count = jnp.where(wrow < 4, nlon[2 * t * n_wave + me], nlon[(2 * t + 1) * n_wave + me])
        quarter = count >> 2
        share = jnp.where((wlane == 0) | (wlane == quarter), 0.5, 1.0)
        share = jnp.where(wlane > quarter, 0.0, share)
        a, e, f, g = (p1 + p2) * share, (p3 + p4) * share, (p1 - p2) * share, (p4 - p3) * share
        folded = jnp.concatenate([a + e, a - e, f + g, f - g], axis=0).astype(BF16)
        first = dot(folded, tab[2 * t], NN)
        second = dot(folded, tab[2 * t + 1], NN)
        row_n = jnp.where(row8 < 4, nlon[2 * t * n_wave + me], nlon[(2 * t + 1) * n_wave + me]).astype(F32)
        row_w = jnp.where(row8 < 4, weights[2 * t * n_wave + me], weights[(2 * t + 1) * n_wave + me])
        scale = 4.0 * (row_w / row_n)
        parts = []
        for part in range(2):
            lanes = slice(part * LANE, (part + 1) * LANE)
            both = [
                jnp.where(even_m, x[part * 16:part * 16 + 8, lanes], x[part * 16 + 8:part * 16 + 16, lanes])
                for x in (first, second)
            ]
            parts.append(jnp.where(row8 < 4, both[0], both[1]) * scale)
        back += parts

    rows = jnp.concatenate(back + [jnp.zeros((LANE - 32, LANE), F32)], axis=0)
    bsend[...] = dot(rows.T.astype(BF16), shift, NN).astype(BF16).reshape(n_wave, slots, LANE)
    for step in range(1, n_wave):
        back_copy(step, me).start()
    brecv[me] = bsend[me]
    for step in range(1, n_wave):
        back_copy(step, peer(n_wave - step)).wait_recv()

    arrived = brecv[...].astype(F32)
    turned = jnp.concatenate(
        [sum(arrived[4 * g + j] for j in range(4)) for g in range(2)], axis=1
    ).astype(BF16)
    placed = dot(turned, rmat[...], NN)
    dcol = iota((slots, depth), 1)
    own_pair = (dcol >> 3) & 7 == iota((slots, depth), 0) >> 1
    rows = jnp.concatenate(
        [jnp.where(own_pair, placed[:, c * depth:(c + 1) * depth], 0.0) for c in range(cols)], axis=0
    ).astype(BF16)
    result = dot(rows, legp[...].reshape(depth, places * LANE), NN)
    for k in range(blocks):
        live = k * LANE + lane16 <= last
        q = blocks - k
        for c in range(cols):
            even = result[c * slots:(c + 1) * slots, k * LANE:(k + 1) * LANE]
            odd = result[c * slots:(c + 1) * slots, q * LANE:(q + 1) * LANE]
            out[c, :, k * LANE:(k + 1) * LANE] = jnp.where(live, jnp.where(even_row, even, odd), 0.0)

    for chunk in range(chunks):
        lev_copy(lev, chunk, across, 0).wait_send()
        lev_copy(lev, chunk, sibling, 1).wait_send()
        lev_copy(across, chunk, sibling, 2).wait_send()
    for step in range(1, n_wave):
        four_copy(step, me).wait_send()
        back_copy(step, me).wait_send()


def fused(spectral, legendre, weights, nlon, assignment):
    cols, slots, kmax = spectral.shape
    lats = legendre.shape[1]
    packed = kmax + LANE
    depth = 4 * slots // 2 * lats
    quarter = -(-(NLONPAD // 4 + 1) // LANE) * LANE
    vmem = pl.BlockSpec(memory_space=pltpu.VMEM)
    dma = pltpu.SemaphoreType.DMA
    return pl.pallas_call(
        fused_kernel,
        out_shape=jax.ShapeDtypeStruct((cols, slots, kmax), F32),
        in_specs=[pl.BlockSpec(memory_space=pltpu.HBM)] * 6,
        out_specs=vmem,
        scratch_shapes=[
            pltpu.SMEM(nlon.shape, I32),
            pltpu.SMEM(weights.shape, F32),
            pltpu.SMEM(assignment.shape, I32),
            pltpu.VMEM((1, assignment.shape[0]), I32),
            pltpu.VMEM(spectral.shape, BF16),
            pltpu.VMEM(legendre.shape, BF16),
            pltpu.VMEM((4, slots // 4, 2 * lats, packed), BF16),
            pltpu.VMEM((packed, LANE), BF16),
            pltpu.VMEM((4, quarter, 2 * LANE), BF16),
            pltpu.VMEM((depth, cols * depth), BF16),
            pltpu.VMEM((LANE, cols * LANE), BF16),
            pltpu.VMEM((8, 8, LANE), F32),
            pltpu.VMEM((8, 8, LANE), F32),
            pltpu.VMEM((8, slots, LANE), BF16),
            pltpu.VMEM((8, slots, LANE), BF16),
            dma((slots // 4 + 5,)),
            dma((3, slots // 4)),
            dma((3, slots // 4)),
            dma((8,)),
            dma((8,)),
            dma((8,)),
            dma((8,)),
        ],
        compiler_params=pltpu.CompilerParams(
            collective_id=0, has_side_effects=True, vmem_limit_bytes=60 * 1024 * 1024
        ),
    )(nlon, weights, assignment, assignment.reshape(1, -1), spectral, legendre)


def solution(mesh):
    def per_shard(spectral, legendre, weights, nlon, assignment):
        fits = (
            mesh.shape["wave"] == 8
            and mesh.shape["lev"] == 4
            and spectral.shape[:2] == (6, 16)
            and legendre.shape[:2] == (16, 8)
            and spectral.shape[2] == TRUNC + 1
        )
        plan = fused if fits else per_device
        return plan(spectral, legendre, weights, nlon, assignment)

    return jax.shard_map(
        per_shard,
        mesh=mesh,
        in_specs=(P("lev", "wave", None), P("wave", "lev", None), P(), P(), P()),
        out_specs=P("lev", "wave", None),
        check_vma=False,
    )
```

```python
import functools
import math

import jax
import jax.numpy as jnp
from jax import lax
from jax.experimental import pallas as pl
from jax.experimental.pallas import tpu as pltpu
from jax.sharding import PartitionSpec as P

TRUNC = 1279
LON_BLOCK = 768
NLONPAD = 5376


def angle_parts(count, waves, starts):
    phase = starts[:, None] % count * waves[None, :] % count
    angle = 2.0 * math.pi * phase.astype(jnp.float32) / count.astype(jnp.float32)
    return (jnp.cos(angle), jnp.sin(angle))


def compose_table(count, waves, coarse_cos, coarse_sin, fine_cos, fine_sin, lon_rows):
    cosine = (
        coarse_cos[:, None, :] * fine_cos[None, :, :]
        - coarse_sin[:, None, :] * fine_sin[None, :, :]
    )
    sine = (
        coarse_sin[:, None, :] * fine_cos[None, :, :]
        + coarse_cos[:, None, :] * fine_sin[None, :, :]
    )
    rows_total = lon_rows.shape[0]
    cosine = cosine.reshape(rows_total, waves.shape[0])
    sine = sine.reshape(rows_total, waves.shape[0])
    usable = (lon_rows[:, None] < count) & (2 * waves[None, :] < count)
    cosine = jnp.where(usable, cosine, jnp.zeros((), jnp.float32))
    sine = jnp.where(usable, -sine, jnp.zeros((), jnp.float32))
    return jnp.concatenate([cosine, sine], axis=1).astype(jnp.bfloat16)


def quadratic(grid):
    fields = grid.reshape(grid.shape[0], grid.shape[1] // 3, 3)
    vort = fields[:, :, 0]
    diverg = fields[:, :, 1]
    temper = fields[:, :, 2]
    stacked = jnp.stack([vort * temper, diverg * temper, vort * diverg], axis=-1)
    return stacked.reshape(grid.shape[0], grid.shape[1]).astype(jnp.bfloat16)


def per_device(spectral, legendre, weights, nlon, assignment):
    wave_index = lax.axis_index("wave")
    lev_index = lax.axis_index("lev")
    slots = legendre.shape[0]
    lat_band = legendre.shape[1]
    kmax_width = legendre.shape[2]
    all_slots = assignment.shape[0]
    own_waves = lax.dynamic_slice_in_dim(assignment, wave_index * slots, slots)
    krange = lax.iota(jnp.int32, kmax_width)
    live_rows = krange[None, :] <= (TRUNC - own_waves)[:, None]
    local = jnp.where(live_rows[None], spectral, jnp.zeros((), jnp.bfloat16))
    spec_all = lax.all_gather(local, "lev", axis=0, tiled=True)
    columns = spec_all.shape[0]
    four_local = jnp.einsum(
        "mlk,cmk->mlc", legendre, spec_all, preferred_element_type=jnp.float32
    ).astype(jnp.bfloat16)
    fourier = lax.all_to_all(four_local, "wave", split_axis=1, concat_axis=0, tiled=True)
    mine = fourier.shape[1]
    half_cols = columns // 2
    fine_rows = lax.iota(jnp.int32, 128)
    coarse_rows = lax.iota(jnp.int32, NLONPAD // 128) * 128
    coarse_step = LON_BLOCK // 128
    lat_index = lev_index * lat_band + wave_index * mine + 0
    count = lax.dynamic_slice_in_dim(nlon, lat_index, 1)[0]
    weight = lax.dynamic_slice_in_dim(weights, lat_index, 1)[0]
    pairs = fourier[:, 0, :].reshape(all_slots, half_cols, 2)
    stacked = jnp.concatenate([pairs[:, :, 0], pairs[:, :, 1]], axis=0)
    fine_cos, fine_sin = angle_parts(count, assignment, fine_rows)
    coarse_cos_all, coarse_sin_all = angle_parts(count, assignment, coarse_rows)

    def lon_block(block_step, total):
        lon_rows = block_step * LON_BLOCK + lax.iota(jnp.int32, LON_BLOCK)
        coarse_cos = lax.dynamic_slice_in_dim(coarse_cos_all, block_step * coarse_step, coarse_step)
        coarse_sin = lax.dynamic_slice_in_dim(coarse_sin_all, block_step * coarse_step, coarse_step)
        table = compose_table(
            count, assignment, coarse_cos, coarse_sin, fine_cos, fine_sin, lon_rows
        )
        grid = 2.0 * jnp.dot(table, stacked, preferred_element_type=jnp.float32)
        products = quadratic(grid)
        return total + lax.dot_general(
            table, products, (((0,), (0,)), ((), ())), preferred_element_type=jnp.float32
        )

    start_total = jnp.zeros((2 * all_slots, half_cols), jnp.float32)
    total = lax.fori_loop(0, NLONPAD // LON_BLOCK, lon_block, start_total)
    back = total * (weight / count.astype(jnp.float32))
    joined = jnp.stack([back[:all_slots], back[all_slots:]], axis=-1).reshape(all_slots, columns)
    analysed_rows = [joined.astype(jnp.bfloat16)]
    analysed = jnp.stack(analysed_rows, axis=1)
    returned = lax.all_to_all(analysed, "wave", split_axis=0, concat_axis=1, tiled=True)
    band_term = jnp.einsum("mlc,mlk->cmk", returned, legendre, preferred_element_type=jnp.float32)
    band_term = jnp.where(live_rows[None], band_term, jnp.zeros((), jnp.float32))
    return lax.psum_scatter(
        band_term.astype(jnp.bfloat16), "lev", scatter_dimension=0, tiled=True
    ).astype(jnp.float32)


MESH = pl.DeviceIdType.MESH
LANE = 128
F32, BF16, I32 = jnp.float32, jnp.bfloat16, jnp.int32
NT = (((1,), (1,)), ((), ()))
NN = (((1,), (0,)), ((), ()))


def dot(a, b, dims):
    return lax.dot_general(a, b, dims, preferred_element_type=F32)


def iota(shape, dim):
    return lax.broadcasted_iota(I32, shape, dim)


def fused_kernel(
    nlon_in, weights_in, waves_in, waves_row, spec_in, leg_in, out,
    nlon, weights, waves_s, waves_v, spec, leg,
    legp, coef, tab, rmat, emat, fsend, frecv, bsend, brecv,
    in_sem, ag_send, ag_recv, f_ssem, f_rsem, b_ssem, b_rsem,
):
    n_wave, n_lev = 8, 4
    far_first = (6, 2, 7, 1, 5, 3, 4)
    chunks = leg.shape[0] // 4
    moves = [
        pltpu.make_async_copy(leg_in.at[pl.ds(4 * i, 4)], leg.at[pl.ds(4 * i, 4)], in_sem.at[i])
        for i in range(chunks)
    ]
    small = ((waves_in, waves_s), (spec_in, spec), (waves_row, waves_v), (nlon_in, nlon), (weights_in, weights))
    moves += [pltpu.make_async_copy(a, b, in_sem.at[chunks + i]) for i, (a, b) in enumerate(small)]
    for move in [moves[chunks]] + moves[:chunks] + moves[chunks + 1:]:
        move.start()
    cols, slots, kmax = spec.shape
    lats = leg.shape[1]
    blocks = kmax // LANE
    places = blocks + 1
    me = lax.axis_index("wave")
    lev = lax.axis_index("lev")
    sibling = lev + 1 - 2 * lax.rem(lev, 2)
    across = lax.rem(lev + 2, n_lev)
    far = lax.rem(sibling + 2, n_lev)

    def peer(step):
        return lax.rem(me + step, n_wave)

    barrier = pltpu.get_barrier_semaphore()
    for step in range(1, n_wave):
        pl.semaphore_signal(barrier, inc=1, device_id=(peer(step), lev), device_id_type=MESH)
    for other in (sibling, across):
        pl.semaphore_signal(barrier, inc=1, device_id=(me, other), device_id_type=MESH)

    def lev_copy(band, chunk, target, sem):
        return pltpu.make_async_remote_copy(
            src_ref=legp.at[band, chunk],
            dst_ref=legp.at[band, chunk],
            send_sem=ag_send.at[sem, chunk],
            recv_sem=ag_recv.at[sem, chunk],
            device_id=(me, target),
            device_id_type=MESH,
        )

    moves[chunks].wait()
    own = [waves_s[me * slots + s] for s in range(slots)]

    def pack_chunk(chunk):
        counts = [
            (jnp.full((lats, LANE), TRUNC + 1, I32) - own[2 * i] + (LANE - 1)) >> 7
            for i in (2 * chunk, 2 * chunk + 1)
        ]
        for p in range(places):
            halves = []
            for h in range(2):
                i = 2 * chunk + h
                if p < blocks:
                    first = leg[2 * i, :, p * LANE:(p + 1) * LANE].astype(F32)
                if p > 0:
                    q = blocks - p
                    second = leg[2 * i + 1, :, q * LANE:(q + 1) * LANE].astype(F32)
                if p == 0:
                    halves.append(first)
                elif p == blocks:
                    halves.append(second)
                else:
                    halves.append(jnp.where(counts[h] > p, first, second))
            legp[lev, chunk, :, p * LANE:(p + 1) * LANE] = jnp.concatenate(halves, axis=0).astype(BF16)

    for chunk in range(chunks):
        moves[chunk].wait()
        pack_chunk(chunk)
        if chunk == 0:
            pl.semaphore_wait(barrier, n_wave - 1 + 2)
        lev_copy(lev, chunk, across, 0).start()
        lev_copy(lev, chunk, sibling, 1).start()

    row16 = iota((slots, LANE), 0)
    lane16 = iota((slots, LANE), 1)
    even_row = row16 & 1 == 0
    last = jnp.zeros((slots, LANE), I32)
    for s in range(slots):
        last = jnp.where(row16 == s, TRUNC - own[s], last)
    zero16 = jnp.zeros((slots, LANE), F32)
    moves[chunks + 1].wait()
    padding = jnp.zeros((LANE - cols * slots, LANE), F32)
    for p in range(places):
        q = blocks - p
        live = jnp.where(even_row, p * LANE, q * LANE) + lane16 <= last
        pieces = []
        for c in range(cols):
            even = spec[c, :, p * LANE:(p + 1) * LANE].astype(F32) if p < blocks else zero16
            odd = spec[c, :, q * LANE:(q + 1) * LANE].astype(F32) if p > 0 else zero16
            pieces.append(jnp.where(live, jnp.where(even_row, even, odd), 0.0))
        piece = jnp.concatenate(pieces + [padding], axis=0)
        coef[p * LANE:(p + 1) * LANE, :] = piece.T.astype(BF16)

    for move in moves[chunks + 2:]:
        move.wait()
    waves = waves_v[...]
    waves_f = waves.astype(F32)

    def forward(chunk):
        lev_copy(across, chunk, across, 0).wait_recv()
        lev_copy(across, chunk, sibling, 2).start()

    def tables(b):
        count = jnp.full((1, LANE), nlon[b * n_wave + me], I32)
        count_f = count.astype(F32)
        inverse = 1.0 / count_f
        row = iota((40, LANE), 0)
        lon = jnp.where(row < 8, row, jnp.where(row < 24, 8 * (row - 8), LANE * (row - 24)))
        whole = lon.astype(F32) * waves_f
        phase = whole - jnp.floor(whole * inverse) * count_f
        phase = jnp.where(phase < 0.0, phase + count_f, phase)
        phase = jnp.where(phase >= count_f, phase - count_f, phase)
        angle = 2.0 * math.pi * phase / count_f
        cosine, sine = jnp.cos(angle), jnp.sin(angle)
        usable = 2 * waves < count
        c8, s8 = cosine[0:8], sine[0:8]
        fine_cos, fine_sin = [], []
        for t in range(16):
            cm, sm = cosine[8 + t:9 + t], sine[8 + t:9 + t]
            fine_cos.append(cm * c8 - sm * s8)
            fine_sin.append(sm * c8 + cm * s8)
        fine_cos = jnp.concatenate(fine_cos, axis=0)
        fine_sin = jnp.concatenate(fine_sin, axis=0)
        for t in range(tab.shape[1] // LANE):
            cq = jnp.where(usable, cosine[24 + t:25 + t], 0.0)
            sq = jnp.where(usable, sine[24 + t:25 + t], 0.0)
            tab[b, t * LANE:(t + 1) * LANE, 0:LANE] = (cq * fine_cos - sq * fine_sin).astype(BF16)
            tab[b, t * LANE:(t + 1) * LANE, LANE:2 * LANE] = (-(sq * fine_cos + cq * fine_sin)).astype(BF16)

    tables(0)
    forward(0)
    tables(1)
    forward(1)
    tables(2)
    tables(3)
    forward(2)

    depth = n_lev * slots // 2 * lats
    rrow = iota((depth, depth), 0)
    rcol = iota((depth, depth), 1)
    band_c = rcol >> 6
    same = (rrow >> 5) == rcol & 7
    base = (band_c >> 1) * 16 + (band_c & 1) * 4
    for c in range(cols):
        hit = same & (rrow & 31 == base + (c % 2) * 8 + (2 - c // 2))
        rmat[:, c * depth:(c + 1) * depth] = jnp.where(hit, 1.0, 0.0).astype(BF16)

    erow = iota((LANE, cols * LANE), 0)
    ecol = iota((LANE, cols * LANE), 1)
    lane_of = ecol & (LANE - 1)
    hit = erow == (ecol >> 7) * slots + (lane_of & (slots - 1))
    emat[...] = jnp.where(hit, 1.0, 0.0).astype(BF16)

    krow, kcol = iota((LANE, LANE), 0), iota((LANE, LANE), 1)
    shift = jnp.where((krow < 32) & (kcol == krow + 32 * lax.rem(me, 4)), 1.0, 0.0).astype(BF16)

    half = slots // 2 * lats
    coef_all = coef[...]
    yrow = iota((half, LANE), 0) >> 3
    ylane = iota((half, LANE), 1)
    mine = (ylane & (slots - 1)) >> 1 == yrow
    srow = iota((n_wave * 8, half), 0)
    scol = iota((n_wave * 8, half), 1)
    same_lat = srow >> 3 == scol & 7

    def synth(band):
        packed = legp[band].reshape(half, places * LANE)
        four = jnp.where(mine, dot(packed, coef_all, NN), 0.0).astype(BF16)
        pick = jnp.where(same_lat & (srow & 7 == band), 1.0, 0.0).astype(BF16)
        return dot(pick, four, NN)

    total = synth(lev)
    for chunk in range(chunks):
        lev_copy(sibling, chunk, sibling, 1).wait_recv()
    total = total + synth(sibling)
    forward(3)
    total = total + synth(across)
    for chunk in range(chunks):
        lev_copy(far, chunk, sibling, 2).wait_recv()
    total = total + synth(far)
    for j in range(n_wave):
        fsend[j] = total[j * 8:(j + 1) * 8]

    def four_copy(step, slot):
        return pltpu.make_async_remote_copy(
            src_ref=fsend.at[peer(step)],
            dst_ref=frecv.at[slot],
            send_sem=f_ssem.at[step],
            recv_sem=f_rsem.at[step],
            device_id=(peer(step), lev),
            device_id_type=MESH,
        )

    def back_copy(step, slot):
        return pltpu.make_async_remote_copy(
            src_ref=bsend.at[peer(step)],
            dst_ref=brecv.at[slot],
            send_sem=b_ssem.at[step],
            recv_sem=b_rsem.at[step],
            device_id=(peer(step), lev),
            device_id_type=MESH,
        )

    for step in far_first:
        four_copy(step, me).start()
    frecv[me] = fsend[me]
    for step in range(1, n_wave):
        four_copy(step, peer(n_wave - step)).wait_recv()

    wide = dot(frecv[...].reshape(n_wave * 8, LANE).astype(BF16), emat[...], NN)
    from_wave = iota((8, LANE), 1) >> 4
    columns = []
    for c in range(cols):
        part = wide[0:8, c * LANE:(c + 1) * LANE]
        for j in range(1, n_wave):
            part = jnp.where(from_wave == j, wide[j * 8:(j + 1) * 8, c * LANE:(c + 1) * LANE], part)
        columns.append(part)
    even_m = waves & 1 == 0
    row8 = iota((8, LANE), 0)
    in_pair = row8 & 3
    nothing = jnp.zeros((8, LANE), F32)
    width = tab.shape[1]
    wrow = iota((8, width), 0)
    wlane = iota((8, width), 1)

    def spread(part, b):
        z, v, h = (columns[2 * f + part][b:b + 1] for f in range(3))
        rows = jnp.where(in_pair == 1, v, jnp.where(in_pair == 2, h, z))
        return jnp.where(row8 >> 2 == b % 2, rows, 0.0)

    back = []
    for t in range(n_lev // 2):
        sums = None
        for b in (2 * t, 2 * t + 1):
            re, im = spread(0, b), spread(1, b)
            lhs = jnp.concatenate(
                [
                    jnp.concatenate([jnp.where(even_m, re, 0.0), jnp.where(even_m, 0.0, re), nothing, nothing], axis=0),
                    jnp.concatenate([nothing, nothing, jnp.where(even_m, im, 0.0), jnp.where(even_m, 0.0, im)], axis=0),
                ],
                axis=1,
            ).astype(BF16)
            term = dot(lhs, tab[b], NT)
            sums = term if sums is None else sums + term
        ce, co, se, so = (sums[g * 8:(g + 1) * 8] for g in range(4))
        p, q, s, d = ce + co, ce - co, se + so, se - so

        def product(x):
            return x * pltpu.roll(x, 7, 0)

        p1, p2, p3, p4 = product(p + s), product(p - s), product(q - d), product(q + d)
        count = jnp.where(wrow < 4, nlon[2 * t * n_wave + me], nlon[(2 * t + 1) * n_wave + me])
        quarter = count >> 2
        share = jnp.where((wlane == 0) | (wlane == quarter), 0.5, 1.0)
        share = jnp.where(wlane > quarter, 0.0, share)
        a, e, f, g = (p1 + p2) * share, (p3 + p4) * share, (p1 - p2) * share, (p4 - p3) * share
        folded = jnp.concatenate([a + e, a - e, f + g, f - g], axis=0).astype(BF16)
        first = dot(folded, tab[2 * t], NN)
        second = dot(folded, tab[2 * t + 1], NN)
        row_n = jnp.where(row8 < 4, nlon[2 * t * n_wave + me], nlon[(2 * t + 1) * n_wave + me]).astype(F32)
        row_w = jnp.where(row8 < 4, weights[2 * t * n_wave + me], weights[(2 * t + 1) * n_wave + me])
        scale = 4.0 * (row_w / row_n)
        parts = []
        for part in range(2):
            lanes = slice(part * LANE, (part + 1) * LANE)
            both = [
                jnp.where(even_m, x[part * 16:part * 16 + 8, lanes], x[part * 16 + 8:part * 16 + 16, lanes])
                for x in (first, second)
            ]
            parts.append(jnp.where(row8 < 4, both[0], both[1]) * scale)
        back += parts

    rows = jnp.concatenate(back + [jnp.zeros((LANE - 32, LANE), F32)], axis=0)
    bsend[...] = dot(rows.T.astype(BF16), shift, NN).astype(BF16).reshape(n_wave, slots, LANE)
    for step in far_first:
        back_copy(step, me).start()
    brecv[me] = bsend[me]
    for step in range(1, n_wave):
        back_copy(step, peer(n_wave - step)).wait_recv()

    arrived = brecv[...].astype(F32)
    turned = jnp.concatenate(
        [sum(arrived[4 * g + j] for j in range(4)) for g in range(2)], axis=1
    ).astype(BF16)
    placed = dot(turned, rmat[...], NN)
    dcol = iota((slots, depth), 1)
    own_pair = (dcol >> 3) & 7 == iota((slots, depth), 0) >> 1
    rows = jnp.concatenate(
        [jnp.where(own_pair, placed[:, c * depth:(c + 1) * depth], 0.0) for c in range(cols)], axis=0
    ).astype(BF16)
    result = dot(rows, legp[...].reshape(depth, places * LANE), NN)
    for k in range(blocks):
        live = k * LANE + lane16 <= last
        q = blocks - k
        for c in range(cols):
            even = result[c * slots:(c + 1) * slots, k * LANE:(k + 1) * LANE]
            odd = result[c * slots:(c + 1) * slots, q * LANE:(q + 1) * LANE]
            out[c, :, k * LANE:(k + 1) * LANE] = jnp.where(live, jnp.where(even_row, even, odd), 0.0)

    for chunk in range(chunks):
        lev_copy(lev, chunk, across, 0).wait_send()
        lev_copy(lev, chunk, sibling, 1).wait_send()
        lev_copy(across, chunk, sibling, 2).wait_send()
    for step in range(1, n_wave):
        four_copy(step, me).wait_send()
        back_copy(step, me).wait_send()


def fused(spectral, legendre, weights, nlon, assignment):
    cols, slots, kmax = spectral.shape
    lats = legendre.shape[1]
    packed = kmax + LANE
    depth = 4 * slots // 2 * lats
    quarter = -(-(NLONPAD // 4 + 1) // LANE) * LANE
    vmem = pl.BlockSpec(memory_space=pltpu.VMEM)
    dma = pltpu.SemaphoreType.DMA
    return pl.pallas_call(
        fused_kernel,
        out_shape=pltpu.VMEM((cols, slots, kmax), F32),
        in_specs=[pl.BlockSpec(memory_space=pltpu.HBM)] * 6,
        out_specs=vmem,
        scratch_shapes=[
            pltpu.SMEM(nlon.shape, I32),
            pltpu.SMEM(weights.shape, F32),
            pltpu.SMEM(assignment.shape, I32),
            pltpu.VMEM((1, assignment.shape[0]), I32),
            pltpu.VMEM(spectral.shape, BF16),
            pltpu.VMEM(legendre.shape, BF16),
            pltpu.VMEM((4, slots // 4, 2 * lats, packed), BF16),
            pltpu.VMEM((packed, LANE), BF16),
            pltpu.VMEM((4, quarter, 2 * LANE), BF16),
            pltpu.VMEM((depth, cols * depth), BF16),
            pltpu.VMEM((LANE, cols * LANE), BF16),
            pltpu.VMEM((8, 8, LANE), F32),
            pltpu.VMEM((8, 8, LANE), F32),
            pltpu.VMEM((8, slots, LANE), BF16),
            pltpu.VMEM((8, slots, LANE), BF16),
            dma((slots // 4 + 5,)),
            dma((3, slots // 4)),
            dma((3, slots // 4)),
            dma((8,)),
            dma((8,)),
            dma((8,)),
            dma((8,)),
        ],
        compiler_params=pltpu.CompilerParams(
            collective_id=0, has_side_effects=True, vmem_limit_bytes=56 * 1024 * 1024
        ),
    )(nlon, weights, assignment, assignment.reshape(1, -1), spectral, legendre)


def solution(mesh):
    def per_shard(spectral, legendre, weights, nlon, assignment):
        fits = (
            mesh.shape["wave"] == 8
            and mesh.shape["lev"] == 4
            and spectral.shape[:2] == (6, 16)
            and legendre.shape[:2] == (16, 8)
            and spectral.shape[2] == TRUNC + 1
        )
        plan = fused if fits else per_device
        return plan(spectral, legendre, weights, nlon, assignment)

    return jax.shard_map(
        per_shard,
        mesh=mesh,
        in_specs=(P("lev", "wave", None), P("wave", "lev", None), P(), P(), P()),
        out_specs=P("lev", "wave", None),
        check_vma=False,
    )
```

```python
import functools
import math

import jax
import jax.numpy as jnp
from jax import lax
from jax.experimental import pallas as pl
from jax.experimental.pallas import tpu as pltpu
from jax.sharding import PartitionSpec as P

TRUNC = 1279
LON_BLOCK = 768
NLONPAD = 5376


def angle_parts(count, waves, starts):
    phase = starts[:, None] % count * waves[None, :] % count
    angle = 2.0 * math.pi * phase.astype(jnp.float32) / count.astype(jnp.float32)
    return (jnp.cos(angle), jnp.sin(angle))


def compose_table(count, waves, coarse_cos, coarse_sin, fine_cos, fine_sin, lon_rows):
    cosine = (
        coarse_cos[:, None, :] * fine_cos[None, :, :]
        - coarse_sin[:, None, :] * fine_sin[None, :, :]
    )
    sine = (
        coarse_sin[:, None, :] * fine_cos[None, :, :]
        + coarse_cos[:, None, :] * fine_sin[None, :, :]
    )
    rows_total = lon_rows.shape[0]
    cosine = cosine.reshape(rows_total, waves.shape[0])
    sine = sine.reshape(rows_total, waves.shape[0])
    usable = (lon_rows[:, None] < count) & (2 * waves[None, :] < count)
    cosine = jnp.where(usable, cosine, jnp.zeros((), jnp.float32))
    sine = jnp.where(usable, -sine, jnp.zeros((), jnp.float32))
    return jnp.concatenate([cosine, sine], axis=1).astype(jnp.bfloat16)


def quadratic(grid):
    fields = grid.reshape(grid.shape[0], grid.shape[1] // 3, 3)
    vort = fields[:, :, 0]
    diverg = fields[:, :, 1]
    temper = fields[:, :, 2]
    stacked = jnp.stack([vort * temper, diverg * temper, vort * diverg], axis=-1)
    return stacked.reshape(grid.shape[0], grid.shape[1]).astype(jnp.bfloat16)


def per_device(spectral, legendre, weights, nlon, assignment):
    wave_index = lax.axis_index("wave")
    lev_index = lax.axis_index("lev")
    slots = legendre.shape[0]
    lat_band = legendre.shape[1]
    kmax_width = legendre.shape[2]
    all_slots = assignment.shape[0]
    own_waves = lax.dynamic_slice_in_dim(assignment, wave_index * slots, slots)
    krange = lax.iota(jnp.int32, kmax_width)
    live_rows = krange[None, :] <= (TRUNC - own_waves)[:, None]
    local = jnp.where(live_rows[None], spectral, jnp.zeros((), jnp.bfloat16))
    spec_all = lax.all_gather(local, "lev", axis=0, tiled=True)
    columns = spec_all.shape[0]
    four_local = jnp.einsum(
        "mlk,cmk->mlc", legendre, spec_all, preferred_element_type=jnp.float32
    ).astype(jnp.bfloat16)
    fourier = lax.all_to_all(four_local, "wave", split_axis=1, concat_axis=0, tiled=True)
    mine = fourier.shape[1]
    half_cols = columns // 2
    fine_rows = lax.iota(jnp.int32, 128)
    coarse_rows = lax.iota(jnp.int32, NLONPAD // 128) * 128
    coarse_step = LON_BLOCK // 128
    lat_index = lev_index * lat_band + wave_index * mine + 0
    count = lax.dynamic_slice_in_dim(nlon, lat_index, 1)[0]
    weight = lax.dynamic_slice_in_dim(weights, lat_index, 1)[0]
    pairs = fourier[:, 0, :].reshape(all_slots, half_cols, 2)
    stacked = jnp.concatenate([pairs[:, :, 0], pairs[:, :, 1]], axis=0)
    fine_cos, fine_sin = angle_parts(count, assignment, fine_rows)
    coarse_cos_all, coarse_sin_all = angle_parts(count, assignment, coarse_rows)

    def lon_block(block_step, total):
        lon_rows = block_step * LON_BLOCK + lax.iota(jnp.int32, LON_BLOCK)
        coarse_cos = lax.dynamic_slice_in_dim(coarse_cos_all, block_step * coarse_step, coarse_step)
        coarse_sin = lax.dynamic_slice_in_dim(coarse_sin_all, block_step * coarse_step, coarse_step)
        table = compose_table(
            count, assignment, coarse_cos, coarse_sin, fine_cos, fine_sin, lon_rows
        )
        grid = 2.0 * jnp.dot(table, stacked, preferred_element_type=jnp.float32)
        products = quadratic(grid)
        return total + lax.dot_general(
            table, products, (((0,), (0,)), ((), ())), preferred_element_type=jnp.float32
        )

    start_total = jnp.zeros((2 * all_slots, half_cols), jnp.float32)
    total = lax.fori_loop(0, NLONPAD // LON_BLOCK, lon_block, start_total)
    back = total * (weight / count.astype(jnp.float32))
    joined = jnp.stack([back[:all_slots], back[all_slots:]], axis=-1).reshape(all_slots, columns)
    analysed_rows = [joined.astype(jnp.bfloat16)]
    analysed = jnp.stack(analysed_rows, axis=1)
    returned = lax.all_to_all(analysed, "wave", split_axis=0, concat_axis=1, tiled=True)
    band_term = jnp.einsum("mlc,mlk->cmk", returned, legendre, preferred_element_type=jnp.float32)
    band_term = jnp.where(live_rows[None], band_term, jnp.zeros((), jnp.float32))
    return lax.psum_scatter(
        band_term.astype(jnp.bfloat16), "lev", scatter_dimension=0, tiled=True
    ).astype(jnp.float32)


MESH = pl.DeviceIdType.MESH
LANE = 128
F32, BF16, I32 = jnp.float32, jnp.bfloat16, jnp.int32
NT = (((1,), (1,)), ((), ()))
NN = (((1,), (0,)), ((), ()))


def dot(a, b, dims):
    return lax.dot_general(a, b, dims, preferred_element_type=F32)


def iota(shape, dim):
    return lax.broadcasted_iota(I32, shape, dim)


def fused_kernel(
    nlon_in, weights_in, waves_in, waves_row, spec_in, leg_in, out,
    nlon, weights, waves_s, waves_v, spec, leg,
    legp, coef, tab, rmat, emat, fsend, frecv, bsend, brecv,
    in_sem, ag_send, ag_recv, f_ssem, f_rsem, b_ssem, b_rsem, met,
):
    n_wave, n_lev = 8, 4
    far_first = (6, 2, 7, 1, 5, 3, 4)
    chunks = leg.shape[0] // 4
    moves = [
        pltpu.make_async_copy(leg_in.at[pl.ds(4 * i, 4)], leg.at[pl.ds(4 * i, 4)], in_sem.at[i])
        for i in range(chunks)
    ]
    small = ((waves_in, waves_s), (spec_in, spec), (waves_row, waves_v), (nlon_in, nlon), (weights_in, weights))
    moves += [pltpu.make_async_copy(a, b, in_sem.at[chunks + i]) for i, (a, b) in enumerate(small)]
    for move in [moves[chunks]] + moves[:chunks] + moves[chunks + 1:]:
        move.start()
    cols, slots, kmax = spec.shape
    lats = leg.shape[1]
    blocks = kmax // LANE
    places = blocks + 1
    me = lax.axis_index("wave")
    lev = lax.axis_index("lev")
    sibling = lev + 1 - 2 * lax.rem(lev, 2)
    across = lax.rem(lev + 2, n_lev)
    far = lax.rem(sibling + 2, n_lev)

    def peer(step):
        return lax.rem(me + step, n_wave)

    partners = (me + 1 - 2 * lax.rem(me, 2), me + 2 - 4 * lax.rem(me // 2, 2), lax.rem(me + 4, n_wave))
    barrier = pltpu.get_barrier_semaphore()
    for other in (sibling, across):
        pl.semaphore_signal(barrier, inc=1, device_id=(me, other), device_id_type=MESH)
    for partner in partners:
        pl.semaphore_signal(barrier, inc=1, device_id=(partner, lev), device_id_type=MESH)

    def greet(turn):
        for axis, partner in enumerate(partners):
            pl.semaphore_signal(met.at[turn, axis], inc=1, device_id=(partner, lev), device_id_type=MESH)

    def met_all(turn):
        for axis in range(len(partners)):
            pl.semaphore_wait(met.at[turn, axis], 1)

    def lev_copy(band, chunk, target, sem):
        return pltpu.make_async_remote_copy(
            src_ref=legp.at[band, chunk],
            dst_ref=legp.at[band, chunk],
            send_sem=ag_send.at[sem, chunk],
            recv_sem=ag_recv.at[sem, chunk],
            device_id=(me, target),
            device_id_type=MESH,
        )

    moves[chunks].wait()
    own = [waves_s[me * slots + s] for s in range(slots)]

    def pack_chunk(chunk):
        counts = [
            (jnp.full((lats, LANE), TRUNC + 1, I32) - own[2 * i] + (LANE - 1)) >> 7
            for i in (2 * chunk, 2 * chunk + 1)
        ]
        for p in range(places):
            halves = []
            for h in range(2):
                i = 2 * chunk + h
                if p < blocks:
                    first = leg[2 * i, :, p * LANE:(p + 1) * LANE].astype(F32)
                if p > 0:
                    q = blocks - p
                    second = leg[2 * i + 1, :, q * LANE:(q + 1) * LANE].astype(F32)
                if p == 0:
                    halves.append(first)
                elif p == blocks:
                    halves.append(second)
                else:
                    halves.append(jnp.where(counts[h] > p, first, second))
            legp[lev, chunk, :, p * LANE:(p + 1) * LANE] = jnp.concatenate(halves, axis=0).astype(BF16)

    for chunk in range(chunks):
        moves[chunk].wait()
        pack_chunk(chunk)
        if chunk == 0:
            pl.semaphore_wait(barrier, 2 + len(partners))
        lev_copy(lev, chunk, across, 0).start()
        lev_copy(lev, chunk, sibling, 1).start()
        if chunk == 0:
            greet(0)

    row16 = iota((slots, LANE), 0)
    lane16 = iota((slots, LANE), 1)
    even_row = row16 & 1 == 0
    last = jnp.zeros((slots, LANE), I32)
    for s in range(slots):
        last = jnp.where(row16 == s, TRUNC - own[s], last)
    zero16 = jnp.zeros((slots, LANE), F32)
    moves[chunks + 1].wait()
    padding = jnp.zeros((LANE - cols * slots, LANE), F32)
    for p in range(places):
        q = blocks - p
        live = jnp.where(even_row, p * LANE, q * LANE) + lane16 <= last
        pieces = []
        for c in range(cols):
            even = spec[c, :, p * LANE:(p + 1) * LANE].astype(F32) if p < blocks else zero16
            odd = spec[c, :, q * LANE:(q + 1) * LANE].astype(F32) if p > 0 else zero16
            pieces.append(jnp.where(live, jnp.where(even_row, even, odd), 0.0))
        piece = jnp.concatenate(pieces + [padding], axis=0)
        coef[p * LANE:(p + 1) * LANE, :] = piece.T.astype(BF16)

    for move in moves[chunks + 2:]:
        move.wait()
    waves = waves_v[...]
    waves_f = waves.astype(F32)

    def forward(chunk):
        lev_copy(across, chunk, across, 0).wait_recv()
        lev_copy(across, chunk, sibling, 2).start()

    def tables(b):
        count = jnp.full((1, LANE), nlon[b * n_wave + me], I32)
        count_f = count.astype(F32)
        inverse = 1.0 / count_f
        row = iota((40, LANE), 0)
        lon = jnp.where(row < 8, row, jnp.where(row < 24, 8 * (row - 8), LANE * (row - 24)))
        whole = lon.astype(F32) * waves_f
        phase = whole - jnp.floor(whole * inverse) * count_f
        phase = jnp.where(phase < 0.0, phase + count_f, phase)
        phase = jnp.where(phase >= count_f, phase - count_f, phase)
        angle = 2.0 * math.pi * phase / count_f
        cosine, sine = jnp.cos(angle), jnp.sin(angle)
        usable = 2 * waves < count
        c8, s8 = cosine[0:8], sine[0:8]
        fine_cos, fine_sin = [], []
        for t in range(16):
            cm, sm = cosine[8 + t:9 + t], sine[8 + t:9 + t]
            fine_cos.append(cm * c8 - sm * s8)
            fine_sin.append(sm * c8 + cm * s8)
        fine_cos = jnp.concatenate(fine_cos, axis=0)
        fine_sin = jnp.concatenate(fine_sin, axis=0)
        for t in range(tab.shape[1] // LANE):
            cq = jnp.where(usable, cosine[24 + t:25 + t], 0.0)
            sq = jnp.where(usable, sine[24 + t:25 + t], 0.0)
            tab[b, t * LANE:(t + 1) * LANE, 0:LANE] = (cq * fine_cos - sq * fine_sin).astype(BF16)
            tab[b, t * LANE:(t + 1) * LANE, LANE:2 * LANE] = (-(sq * fine_cos + cq * fine_sin)).astype(BF16)

    tables(0)
    forward(0)
    met_all(0)
    greet(1)
    tables(1)
    forward(1)
    tables(2)
    tables(3)
    forward(2)

    depth = n_lev * slots // 2 * lats
    rrow = iota((depth, depth), 0)
    rcol = iota((depth, depth), 1)
    band_c = rcol >> 6
    same = (rrow >> 5) == rcol & 7
    base = (band_c >> 1) * 16 + (band_c & 1) * 4
    for c in range(cols):
        hit = same & (rrow & 31 == base + (c % 2) * 8 + (2 - c // 2))
        rmat[:, c * depth:(c + 1) * depth] = jnp.where(hit, 1.0, 0.0).astype(BF16)

    erow = iota((LANE, cols * LANE), 0)
    ecol = iota((LANE, cols * LANE), 1)
    lane_of = ecol & (LANE - 1)
    hit = erow == (ecol >> 7) * slots + (lane_of & (slots - 1))
    emat[...] = jnp.where(hit, 1.0, 0.0).astype(BF16)

    krow, kcol = iota((LANE, LANE), 0), iota((LANE, LANE), 1)
    shift = jnp.where((krow < 32) & (kcol == krow + 32 * lax.rem(me, 4)), 1.0, 0.0).astype(BF16)

    half = slots // 2 * lats
    coef_all = coef[...]
    yrow = iota((half, LANE), 0) >> 3
    ylane = iota((half, LANE), 1)
    mine = (ylane & (slots - 1)) >> 1 == yrow
    srow = iota((n_wave * 8, half), 0)
    scol = iota((n_wave * 8, half), 1)
    same_lat = srow >> 3 == scol & 7

    def synth(band):
        packed = legp[band].reshape(half, places * LANE)
        four = jnp.where(mine, dot(packed, coef_all, NN), 0.0).astype(BF16)
        pick = jnp.where(same_lat & (srow & 7 == band), 1.0, 0.0).astype(BF16)
        return dot(pick, four, NN)

    total = synth(lev)
    for chunk in range(chunks):
        lev_copy(sibling, chunk, sibling, 1).wait_recv()
    total = total + synth(sibling)
    forward(3)
    total = total + synth(across)
    for chunk in range(chunks):
        lev_copy(far, chunk, sibling, 2).wait_recv()
    total = total + synth(far)
    for j in range(n_wave):
        fsend[j] = total[j * 8:(j + 1) * 8]

    def four_copy(step, slot):
        return pltpu.make_async_remote_copy(
            src_ref=fsend.at[peer(step)],
            dst_ref=frecv.at[slot],
            send_sem=f_ssem.at[step],
            recv_sem=f_rsem.at[step],
            device_id=(peer(step), lev),
            device_id_type=MESH,
        )

    def back_copy(step, slot):
        return pltpu.make_async_remote_copy(
            src_ref=bsend.at[peer(step)],
            dst_ref=brecv.at[slot],
            send_sem=b_ssem.at[step],
            recv_sem=b_rsem.at[step],
            device_id=(peer(step), lev),
            device_id_type=MESH,
        )

    met_all(1)
    for step in far_first:
        four_copy(step, me).start()
    frecv[me] = fsend[me]
    for step in range(1, n_wave):
        four_copy(step, peer(n_wave - step)).wait_recv()

    wide = dot(frecv[...].reshape(n_wave * 8, LANE).astype(BF16), emat[...], NN)
    from_wave = iota((8, LANE), 1) >> 4
    columns = []
    for c in range(cols):
        part = wide[0:8, c * LANE:(c + 1) * LANE]
        for j in range(1, n_wave):
            part = jnp.where(from_wave == j, wide[j * 8:(j + 1) * 8, c * LANE:(c + 1) * LANE], part)
        columns.append(part)
    even_m = waves & 1 == 0
    row8 = iota((8, LANE), 0)
    in_pair = row8 & 3
    nothing = jnp.zeros((8, LANE), F32)
    width = tab.shape[1]
    wrow = iota((8, width), 0)
    wlane = iota((8, width), 1)

    def spread(part, b):
        z, v, h = (columns[2 * f + part][b:b + 1] for f in range(3))
        rows = jnp.where(in_pair == 1, v, jnp.where(in_pair == 2, h, z))
        return jnp.where(row8 >> 2 == b % 2, rows, 0.0)

    back = []
    for t in range(n_lev // 2):
        sums = None
        for b in (2 * t, 2 * t + 1):
            re, im = spread(0, b), spread(1, b)
            lhs = jnp.concatenate(
                [
                    jnp.concatenate([jnp.where(even_m, re, 0.0), jnp.where(even_m, 0.0, re), nothing, nothing], axis=0),
                    jnp.concatenate([nothing, nothing, jnp.where(even_m, im, 0.0), jnp.where(even_m, 0.0, im)], axis=0),
                ],
                axis=1,
            ).astype(BF16)
            term = dot(lhs, tab[b], NT)
            sums = term if sums is None else sums + term
        ce, co, se, so = (sums[g * 8:(g + 1) * 8] for g in range(4))
        p, q, s, d = ce + co, ce - co, se + so, se - so

        def product(x):
            return x * pltpu.roll(x, 7, 0)

        p1, p2, p3, p4 = product(p + s), product(p - s), product(q - d), product(q + d)
        count = jnp.where(wrow < 4, nlon[2 * t * n_wave + me], nlon[(2 * t + 1) * n_wave + me])
        quarter = count >> 2
        share = jnp.where((wlane == 0) | (wlane == quarter), 0.5, 1.0)
        share = jnp.where(wlane > quarter, 0.0, share)
        a, e, f, g = (p1 + p2) * share, (p3 + p4) * share, (p1 - p2) * share, (p4 - p3) * share
        folded = jnp.concatenate([a + e, a - e, f + g, f - g], axis=0).astype(BF16)
        first = dot(folded, tab[2 * t], NN)
        second = dot(folded, tab[2 * t + 1], NN)
        row_n = jnp.where(row8 < 4, nlon[2 * t * n_wave + me], nlon[(2 * t + 1) * n_wave + me]).astype(F32)
        row_w = jnp.where(row8 < 4, weights[2 * t * n_wave + me], weights[(2 * t + 1) * n_wave + me])
        scale = 4.0 * (row_w / row_n)
        parts = []
        for part in range(2):
            lanes = slice(part * LANE, (part + 1) * LANE)
            both = [
                jnp.where(even_m, x[part * 16:part * 16 + 8, lanes], x[part * 16 + 8:part * 16 + 16, lanes])
                for x in (first, second)
            ]
            parts.append(jnp.where(row8 < 4, both[0], both[1]) * scale)
        back += parts

    rows = jnp.concatenate(back + [jnp.zeros((LANE - 32, LANE), F32)], axis=0)
    bsend[...] = dot(rows.T.astype(BF16), shift, NN).astype(BF16).reshape(n_wave, slots, LANE)
    for step in far_first:
        back_copy(step, me).start()
    brecv[me] = bsend[me]
    for step in range(1, n_wave):
        back_copy(step, peer(n_wave - step)).wait_recv()

    arrived = brecv[...].astype(F32)
    turned = jnp.concatenate(
        [sum(arrived[4 * g + j] for j in range(4)) for g in range(2)], axis=1
    ).astype(BF16)
    placed = dot(turned, rmat[...], NN)
    dcol = iota((slots, depth), 1)
    own_pair = (dcol >> 3) & 7 == iota((slots, depth), 0) >> 1
    rows = jnp.concatenate(
        [jnp.where(own_pair, placed[:, c * depth:(c + 1) * depth], 0.0) for c in range(cols)], axis=0
    ).astype(BF16)
    result = dot(rows, legp[...].reshape(depth, places * LANE), NN)
    for k in range(blocks):
        live = k * LANE + lane16 <= last
        q = blocks - k
        for c in range(cols):
            even = result[c * slots:(c + 1) * slots, k * LANE:(k + 1) * LANE]
            odd = result[c * slots:(c + 1) * slots, q * LANE:(q + 1) * LANE]
            out[c, :, k * LANE:(k + 1) * LANE] = jnp.where(live, jnp.where(even_row, even, odd), 0.0)

    for chunk in range(chunks):
        lev_copy(lev, chunk, across, 0).wait_send()
        lev_copy(lev, chunk, sibling, 1).wait_send()
        lev_copy(across, chunk, sibling, 2).wait_send()
    for step in range(1, n_wave):
        four_copy(step, me).wait_send()
        back_copy(step, me).wait_send()


def fused(spectral, legendre, weights, nlon, assignment):
    cols, slots, kmax = spectral.shape
    lats = legendre.shape[1]
    packed = kmax + LANE
    depth = 4 * slots // 2 * lats
    quarter = -(-(NLONPAD // 4 + 1) // LANE) * LANE
    vmem = pl.BlockSpec(memory_space=pltpu.VMEM)
    dma = pltpu.SemaphoreType.DMA
    return pl.pallas_call(
        fused_kernel,
        out_shape=pltpu.VMEM((cols, slots, kmax), F32),
        in_specs=[pl.BlockSpec(memory_space=pltpu.HBM)] * 6,
        out_specs=vmem,
        scratch_shapes=[
            pltpu.SMEM(nlon.shape, I32),
            pltpu.SMEM(weights.shape, F32),
            pltpu.SMEM(assignment.shape, I32),
            pltpu.VMEM((1, assignment.shape[0]), I32),
            pltpu.VMEM(spectral.shape, BF16),
            pltpu.VMEM(legendre.shape, BF16),
            pltpu.VMEM((4, slots // 4, 2 * lats, packed), BF16),
            pltpu.VMEM((packed, LANE), BF16),
            pltpu.VMEM((4, quarter, 2 * LANE), BF16),
            pltpu.VMEM((depth, cols * depth), BF16),
            pltpu.VMEM((LANE, cols * LANE), BF16),
            pltpu.VMEM((8, 8, LANE), F32),
            pltpu.VMEM((8, 8, LANE), F32),
            pltpu.VMEM((8, slots, LANE), BF16),
            pltpu.VMEM((8, slots, LANE), BF16),
            dma((slots // 4 + 5,)),
            dma((3, slots // 4)),
            dma((3, slots // 4)),
            dma((8,)),
            dma((8,)),
            dma((8,)),
            dma((8,)),
            pltpu.SemaphoreType.REGULAR((2, 3)),
        ],
        compiler_params=pltpu.CompilerParams(
            collective_id=0, has_side_effects=True, vmem_limit_bytes=56 * 1024 * 1024
        ),
    )(nlon, weights, assignment, assignment.reshape(1, -1), spectral, legendre)


def solution(mesh):
    def per_shard(spectral, legendre, weights, nlon, assignment):
        fits = (
            mesh.shape["wave"] == 8
            and mesh.shape["lev"] == 4
            and spectral.shape[:2] == (6, 16)
            and legendre.shape[:2] == (16, 8)
            and spectral.shape[2] == TRUNC + 1
        )
        plan = fused if fits else per_device
        return plan(spectral, legendre, weights, nlon, assignment)

    return jax.shard_map(
        per_shard,
        mesh=mesh,
        in_specs=(P("lev", "wave", None), P("wave", "lev", None), P(), P(), P()),
        out_specs=P("lev", "wave", None),
        check_vma=False,
    )
```
